512 devices in a mesh: dp: 64 (over y_lo, x, z), tensor: 8 (over y_hi, core).
Axes of the slice: x: 4, y: 8 (y_hi: 4, y_lo: 2; y = y_hi * 2 + y_lo), z: 8, core: 2. Of those that a mesh axis runs over, the one named last changes fastest.
Arguments:
- normalized_input: bfloat16 [4096, 16384], P(None, 'dp'), may hold values from -16 to 16
- quantized_weight_codes: bfloat16 [4096, 8, 128], P('dp', 'tensor'), may hold values from -0.09375 to 0.09375
- exponents: int32 [64, 8], P('dp', 'tensor'), may hold values from -2 to 1
- queries: bfloat16 [16384, 8, 512], P('dp', 'tensor'), may hold values from -64 to 64
- rotated_keys: bfloat16 [16384, 8, 128], P('dp', 'tensor'), may hold values from -4 to 4
- doc_start: int32 [16384], P('dp'), may hold values from 0 to 16383, as said below
- output_cotangent: bfloat16 [16384, 8, 512], P('dp', 'tensor'), may hold values from -6 to 6
Outputs:
- attention_output: bfloat16 [16384, 8, 512], P('dp', 'tensor')
- query_gradient: bfloat16 [16384, 8, 512], P('dp', 'tensor')
- d_keys: bfloat16 [16384, 8, 128], P('dp', 'tensor')
- d_input: bfloat16 [4096, 16384], P('tensor', 'dp')
- projection_gradient: float32 [4096, 8, 128], P('dp', 'tensor')
The draws below stay inside these ranges and needn't reach their ends.
Inputs may be any that keep to these rules, and one draw needn't show every extreme that they name: doc_start[s] is the first position of the document holding token s: it never falls, doc_start[s] <= s, doc_start[doc_start[s]] = doc_start[s], and s - doc_start[s] <= 1023, with equality for some token in every draw.
All inputs are finite; a program needn't handle non-finite values.
Results may differ from the reference program's by a relative error of at most 0.017.
Values may be sent and summed in bfloat16 or wider, within the bound.
No kernel may reach another device: no remote copies, remote signals or barrier semaphores. Data moves between devices by JAX's collectives and lax.ppermute only.
A program may use at most 64 MiB of HBM per device.

```python
import math
import jax
import jax.numpy as jnp
import numpy as np
from jax import lax

INPUT_FEATURES = 4096
KEY_VALUE_HEADS = 8
QUERY_PER_KEY = 4
HEAD_WIDTH = 128
TOK_DEV = 256
SPAN = 4
SEQUENCE_TOKENS = 16384
LONGEST_LENGTH = 1024
SCALE_BLOCKS = 64
N_DP = 64
N_TENSOR = 8


def document_starts(key):
    key = jax.random.fold_in(key, 101)
    lengths = jax.random.randint(key, (SEQUENCE_TOKENS,), 2, LONGEST_LENGTH + 1, dtype=jnp.int32)
    leading = jax.random.randint(jax.random.fold_in(key, 7), (), 2, TOK_DEV, dtype=jnp.int32)
    lengths = lengths.at[0].set(leading).at[1].set(LONGEST_LENGTH)
    begins = (jnp.cumsum(lengths) - lengths).astype(jnp.int32)
    marks = jnp.zeros((SEQUENCE_TOKENS,), jnp.int32).at[begins].set(1, mode='drop')
    places = jnp.arange(SEQUENCE_TOKENS, dtype=jnp.int32)
    return lax.cummax(jnp.where(marks > 0, places, 0), axis=0)


def key_field(key):
    normalized_part = jnp.clip(jax.random.normal(jax.random.fold_in(key, 11), (SEQUENCE_TOKENS, KEY_VALUE_HEADS, HEAD_WIDTH), jnp.float32), -4.0, 4.0)
    return normalized_part


def draw_doc_start(key, part):
    return document_starts(key)


def draw_rotated_keys(key, part):
    normalized_part = key_field(key)
    return normalized_part.astype(jnp.bfloat16)


def draw_queries(key, part):
    local_key_rows = jax.random.fold_in(key, 5)
    return (1.5 * jnp.clip(jax.random.normal(local_key_rows, (SEQUENCE_TOKENS, KEY_VALUE_HEADS, QUERY_PER_KEY * HEAD_WIDTH), jnp.float32), -4.0, 4.0)).astype(jnp.bfloat16)


def place_ends(values, rng, smallest, high):
    dims = values.shape
    spot = [jax.random.randint(jax.random.fold_in(rng, axis), (), 0, dims[axis]) for axis in range(len(dims))]
    values = values.at[tuple(spot)].set(smallest)
    longest = dims.index(max(dims))
    spot[longest] = (spot[longest] + 1) % dims[longest]
    return values.at[tuple(spot)].set(high)


def with_spikes(values, own_key, source, target, blocks, factor):
    def block_of(axis_at):
        return (jnp.arange(values.shape[axis_at]) // (values.shape[axis_at] // blocks)).reshape((-1,) + (1,) * (values.ndim - 1 - axis_at))

    one_side = jax.random.permutation(own_key, blocks)[block_of(target)]
    other_side = (block_of(target) + blocks // 2) % blocks
    return jnp.where((block_of(source) == one_side) | (block_of(source) == other_side), factor * values, values)


def level_of(stream_key, shape, pieces, smallest, top_value):
    loudness = 1.0
    for dim, blocks in pieces:
        heights = jax.random.uniform(jax.random.fold_in(jax.random.fold_in(stream_key, 6), dim), (blocks,), jnp.float32, smallest / len(pieces), top_value / len(pieces))
        loudness = loudness * jnp.repeat(jnp.exp(heights), shape[dim] // blocks).reshape((-1,) + (1,) * (len(shape) - 1 - dim))
    return loudness


def scatter_about(own_key, dims, width, reach, split=(), kind=jnp.bfloat16):
    values = jax.random.normal(own_key, dims, jnp.float32) * width
    if len(split) > 0:
        values = level_of(own_key, dims, split, -0.22, 0.18) * values
    return jnp.clip(values, min=-reach, max=reach).astype(kind)


def noise_with(stream_key, shape, scale, limit, split, heavy, held_as=jnp.bfloat16):
    values = scale * jax.random.normal(stream_key, shape, jnp.float32)
    if split:
        values = values * level_of(stream_key, shape, split, -0.22, 0.18)
    return jnp.clip(with_spikes(values, jax.random.fold_in(stream_key, 3), *heavy), -limit, limit).astype(held_as)


def setup_inputs(seed: int = 0) -> dict:
    seeds = jax.random.split(jax.random.key(seed), 8)
    return {
        "normalized_input": noise_with(seeds[0], (INPUT_FEATURES, SEQUENCE_TOKENS), 1.0, 16.0, ((1, 64),), (1, 0, 64, 4.0)),
        "quantized_weight_codes": scatter_about(seeds[1], (INPUT_FEATURES, KEY_VALUE_HEADS, HEAD_WIDTH), INPUT_FEATURES ** -0.5, 0.09375, ((0, 64), (1, 8))),
        "exponents": place_ends(jax.random.randint(seeds[2], (SCALE_BLOCKS, KEY_VALUE_HEADS), -2, 2), jax.random.fold_in(seeds[2], 1), -2, 1).astype(jnp.int32),
        "queries": draw_queries(jax.random.fold_in(seeds[7], 71), 0),
        "rotated_keys": draw_rotated_keys(jax.random.fold_in(seeds[7], 71), 0),
        "doc_start": draw_doc_start(jax.random.fold_in(seeds[7], 71), 0),
        "output_cotangent": scatter_about(seeds[6], (SEQUENCE_TOKENS, KEY_VALUE_HEADS, QUERY_PER_KEY * HEAD_WIDTH), 1.0, 6.0, ((0, 64), (1, 8))),
    }


powers_table = np.array([0.25, 0.5, 1.0, 2.0], dtype=np.float32)

def block_scale(exponents):
    levels = jnp.arange(4, dtype=jnp.int32) - 2
    picked = (exponents[..., None] == levels).astype(jnp.float32)
    return lax.optimization_barrier(jnp.sum(picked * jnp.asarray(powers_table, dtype=jnp.float32), axis=-1))

def dequantize(quantized_weight_codes, exponents):
    scales = block_scale(exponents)
    repeat_rows = quantized_weight_codes.shape[0] // exponents.shape[0]
    row_scales = jnp.repeat(scales, repeat_rows, axis=0)
    return (quantized_weight_codes.astype(jnp.float32) * row_scales[:, :, None]).astype(jnp.bfloat16)

def attend(query_rows, key_window, value_window, grad_rows, query_pos, key_pos, first_pos):
    row_count, head_count, q_width = query_rows.shape
    head_size = key_window.shape[-1]
    group_size = q_width // head_size
    factor = 1.0 / math.sqrt(head_size)
    q_heads = query_rows.astype(jnp.float32).reshape(row_count, head_count, group_size, head_size)
    g_heads = grad_rows.astype(jnp.float32).reshape(row_count, head_count, group_size, head_size)
    key_float = key_window.astype(jnp.float32)
    value_float = value_window.astype(jnp.float32)
    scores = jnp.einsum('thge,she->thgs', q_heads, key_float) * factor
    allowed = (key_pos[None, :] >= first_pos[:, None]) & (key_pos[None, :] <= query_pos[:, None])
    allowed = allowed[:, None, None, :]
    masked = jnp.where(allowed, scores, -1e+30)
    row_top = lax.optimization_barrier(jnp.max(masked, axis=-1, keepdims=True))
    row_total = lax.optimization_barrier(jnp.sum(jnp.where(allowed, jnp.exp(masked - row_top), 0.0), axis=-1, keepdims=True))
    log_total = row_top + jnp.log(row_total)
    weights_bf = lax.optimization_barrier(jnp.where(allowed, jnp.exp(masked - log_total), 0.0).astype(jnp.bfloat16))
    weights_float = weights_bf.astype(jnp.float32)
    attn_rows = lax.optimization_barrier(jnp.einsum('thgs,she->thge', weights_float, value_float).astype(jnp.bfloat16))
    row_delta = lax.optimization_barrier(jnp.sum(g_heads * attn_rows.astype(jnp.float32), axis=-1, keepdims=True))
    d_weights = jnp.einsum('thge,she->thgs', g_heads, value_float)
    d_scores = lax.optimization_barrier((weights_float * (d_weights - row_delta) * factor).astype(jnp.bfloat16))
    d_float = d_scores.astype(jnp.float32)
    query_gradient = jnp.einsum('thgs,she->thge', d_float, key_float).astype(jnp.bfloat16)
    d_key = jnp.einsum('thgs,thge->she', d_float, q_heads)
    d_value = jnp.einsum('thgs,thge->she', weights_float, g_heads)
    return (attn_rows.reshape(row_count, head_count, q_width), query_gradient.reshape(row_count, head_count, q_width), d_key, d_value)

def reference(normalized_input, quantized_weight_codes, exponents, queries, rotated_keys, doc_start, output_cotangent):
    weight_matrix = dequantize(quantized_weight_codes, exponents)
    flattened_weight = weight_matrix.reshape(INPUT_FEATURES, KEY_VALUE_HEADS * HEAD_WIDTH)
    projected_values = jnp.dot(normalized_input.T, flattened_weight, preferred_element_type=jnp.float32).astype(jnp.bfloat16).reshape(SEQUENCE_TOKENS, KEY_VALUE_HEADS, HEAD_WIDTH)
    window = (SPAN + 1) * TOK_DEV
    padded_keys = jnp.concatenate([jnp.zeros((LONGEST_LENGTH, KEY_VALUE_HEADS, HEAD_WIDTH), jnp.bfloat16), rotated_keys], axis=0)
    padded_values = jnp.concatenate([jnp.zeros((LONGEST_LENGTH, KEY_VALUE_HEADS, HEAD_WIDTH), jnp.bfloat16), projected_values], axis=0)

    def block_step(running, block_id):
        key_grad, value_grad = running
        first_row = (block_id * TOK_DEV).astype(jnp.int32)
        query_block = lax.dynamic_slice_in_dim(queries, first_row, TOK_DEV, 0)
        grad_block = lax.dynamic_slice_in_dim(output_cotangent, first_row, TOK_DEV, 0)
        start_block = lax.dynamic_slice_in_dim(doc_start, first_row, TOK_DEV, 0)
        key_block = lax.dynamic_slice_in_dim(padded_keys, first_row, window, 0)
        value_block = lax.dynamic_slice_in_dim(padded_values, first_row, window, 0)
        query_pos = first_row + jnp.arange(TOK_DEV, dtype=jnp.int32)
        key_pos = first_row - LONGEST_LENGTH + jnp.arange(window, dtype=jnp.int32)
        attn_rows, query_grad, d_key, d_value = attend(query_block, key_block, value_block, grad_block, query_pos, key_pos, start_block)
        key_grad = lax.dynamic_update_slice_in_dim(key_grad, lax.dynamic_slice_in_dim(key_grad, first_row, window, 0) + d_key, first_row, 0)
        value_grad = lax.dynamic_update_slice_in_dim(value_grad, lax.dynamic_slice_in_dim(value_grad, first_row, window, 0) + d_value, first_row, 0)
        return ((key_grad, value_grad), (attn_rows, query_grad))
    zeroed_gradient = jnp.zeros((SEQUENCE_TOKENS + LONGEST_LENGTH, KEY_VALUE_HEADS, HEAD_WIDTH), jnp.float32)
    block_ids = jnp.arange(N_DP, dtype=jnp.int32)
    (key_grad, value_grad), (attention_blocks, query_gradients) = lax.scan(block_step, (zeroed_gradient, zeroed_gradient), block_ids)
    attention_output = attention_blocks.reshape(SEQUENCE_TOKENS, KEY_VALUE_HEADS, QUERY_PER_KEY * HEAD_WIDTH)
    query_gradient = query_gradients.reshape(SEQUENCE_TOKENS, KEY_VALUE_HEADS, QUERY_PER_KEY * HEAD_WIDTH)
    d_keys = key_grad[LONGEST_LENGTH:].astype(jnp.bfloat16)
    value_gradients = value_grad[LONGEST_LENGTH:].astype(jnp.bfloat16)
    flattened_values = value_gradients.reshape(SEQUENCE_TOKENS, KEY_VALUE_HEADS * HEAD_WIDTH)
    projection_gradient = jnp.dot(normalized_input, flattened_values, preferred_element_type=jnp.float32).reshape(INPUT_FEATURES, KEY_VALUE_HEADS, HEAD_WIDTH)
    head_rank_index = KEY_VALUE_HEADS // N_TENSOR
    input_sum = jnp.zeros((INPUT_FEATURES, SEQUENCE_TOKENS), jnp.float32)
    for tensor_rank in range(N_TENSOR):
        col_lower = tensor_rank * head_rank_index * HEAD_WIDTH
        col_upper = col_lower + head_rank_index * HEAD_WIDTH
        partial_grad = jnp.dot(flattened_weight[:, col_lower:col_upper], flattened_values[:, col_lower:col_upper].T, preferred_element_type=jnp.float32).astype(jnp.bfloat16)
        input_sum = input_sum + lax.optimization_barrier(partial_grad).astype(jnp.float32)
    d_input = input_sum.astype(jnp.bfloat16)
    return (attention_output, query_gradient, d_keys, d_input, projection_gradient)
```

```python
import math

import jax
import jax.numpy as jnp
import numpy as np
from jax import lax
from jax.sharding import PartitionSpec as P

SPAN = 4
Z = 8
YX = 8
F32 = jnp.float32
BF16 = jnp.bfloat16

powers_table = np.array([0.25, 0.5, 1.0, 2.0], dtype=np.float32)

Z_GROUPS = [[a * Z + z for z in range(Z)] for a in range(YX)]
YX_GROUPS = [[a * Z + z for a in range(YX)] for z in range(Z)]


def shifted(value, steps):
    count = lax.axis_size("dp")
    first, last = (max(0, -steps), min(count, count - steps))
    return lax.ppermute(value, "dp", [(source, source + steps) for source in range(first, last)])


def swap_all(value, groups):
    return lax.all_to_all(value, "dp", 0, 0, tiled=True, axis_index_groups=groups)


def copies(value, count):
    return jnp.broadcast_to(value[None], (count,) + value.shape).reshape(
        (count * value.shape[0],) + value.shape[1:]
    )


def dequantize(codes, exponent):
    levels = jnp.arange(4, dtype=jnp.int32) - 2
    scale = jnp.sum((exponent == levels).astype(F32) * jnp.asarray(powers_table))
    return (codes.astype(F32) * scale).astype(BF16)


def transposed_heads(value):
    pairs = []
    for a in range(YX):
        for z in range(Z):
            for h in range(8):
                pairs.append(((a * Z + z) * 8 + h, (h * Z + z) * 8 + a))
    return lax.ppermute(value, ("dp", "tensor"), pairs)


def body(x, codes, exponents, queries, keys, doc_start, cotangent):
    feat, tok = x.shape
    width = keys.shape[2]
    group = queries.shape[2] // width
    factor = 1.0 / math.sqrt(width)
    dp_index = lax.axis_index("dp")

    key_own = keys[:, 0, :]
    w_own = dequantize(codes[:, 0, :], exponents[0, 0])
    w_block = swap_all(copies(w_own, Z), Z_GROUPS)
    w_swapped = transposed_heads(w_own)

    def window(own, halo):
        return jnp.concatenate(halo[::-1] + [own], axis=0)

    key_window = window(key_own, [shifted(key_own, s) for s in range(1, SPAN + 1)])
    w_full = swap_all(copies(w_block, YX), YX_GROUPS)

    def rows_of(arr):
        return jnp.concatenate(
            [arr[:, 0, g * width : (g + 1) * width] for g in range(group)], axis=0
        )

    def lanes_of(arr):
        return jnp.concatenate([arr[g * tok : (g + 1) * tok] for g in range(group)], axis=1)[
            :, None, :
        ]

    q_rows = rows_of(queries)
    g_rows = rows_of(cotangent)
    query_pos = dp_index * tok + jnp.arange(tok, dtype=jnp.int32)
    key_pos = (dp_index - SPAN) * tok + jnp.arange((SPAN + 1) * tok, dtype=jnp.int32)
    allowed = (key_pos[None, :] >= doc_start[:, None]) & (key_pos[None, :] <= query_pos[:, None])

    scores = lax.dot_general(
        q_rows, key_window, (((1,), (1,)), ((), ())), preferred_element_type=F32
    ).reshape(group, tok, -1)
    masked = jnp.where(allowed[None], scores * factor, -1e30)
    row_top = jnp.max(masked, axis=-1, keepdims=True)
    row_total = jnp.sum(jnp.exp(masked - row_top), axis=-1, keepdims=True)
    log_total = row_top + jnp.log(row_total)
    probs = jnp.exp(masked - log_total).astype(BF16).reshape(group * tok, -1)
    dv_window = lax.dot_general(
        probs, g_rows, (((0,), (0,)), ((), ())), preferred_element_type=F32
    )

    def halo_sum(grads):
        def piece(offset):
            begin = (SPAN - offset) * tok
            return grads[begin : begin + tok]

        total = piece(0)
        for offset in range(1, SPAN + 1):
            total = total + shifted(piece(offset).astype(BF16), -offset).astype(F32)
        return total.astype(BF16)

    dv_own = halo_sum(dv_window)

    v_own = lax.dot_general(
        x, w_full, (((0,), (0,)), ((), ())), preferred_element_type=F32
    ).astype(BF16)
    value_window = window(v_own, [shifted(v_own, s) for s in range(1, SPAN + 1)])

    dw_part = lax.dot_general(
        x, dv_own, (((1,), (0,)), ((), ())), preferred_element_type=F32
    ).astype(BF16)
    dw_block = swap_all(dw_part, YX_GROUPS).reshape(YX, feat // YX, width)
    dw_block = jnp.sum(dw_block.astype(F32), axis=0).astype(BF16)
    dw_own = swap_all(dw_block, Z_GROUPS).reshape(Z, feat // (YX * Z), width)
    projection_gradient = jnp.sum(dw_own.astype(F32), axis=0)[:, None, :]

    w_rows = swap_all(copies(swap_all(copies(w_swapped, Z), Z_GROUPS), YX), YX_GROUPS)
    w_rows = w_rows.reshape(8, feat // 8, width)
    dv_heads = lax.all_to_all(copies(dv_own, 8), "tensor", 0, 0, tiled=True)
    dv_heads = dv_heads.reshape(8, tok, width)
    d_input = jnp.zeros((feat // 8, tok), F32)
    for h in range(8):
        d_input = d_input + lax.dot_general(
            w_rows[h], dv_heads[h], (((1,), (1,)), ((), ())), preferred_element_type=F32
        )
    d_input = d_input.astype(BF16)

    attn = lax.dot_general(
        probs, value_window, (((1,), (0,)), ((), ())), preferred_element_type=F32
    ).astype(BF16)
    delta = jnp.sum(g_rows.astype(F32) * attn.astype(F32), axis=-1, keepdims=True)
    dprob = lax.dot_general(
        g_rows, value_window, (((1,), (1,)), ((), ())), preferred_element_type=F32
    )
    dscore = (probs.astype(F32) * (dprob - delta) * factor).astype(BF16)
    dq = lax.dot_general(
        dscore, key_window, (((1,), (0,)), ((), ())), preferred_element_type=F32
    ).astype(BF16)
    dk_window = lax.dot_general(
        dscore, q_rows, (((0,), (0,)), ((), ())), preferred_element_type=F32
    )
    d_keys = halo_sum(dk_window)[:, None, :]
    return (lanes_of(attn), lanes_of(dq), d_keys, d_input, projection_gradient)


def solution(mesh):
    in_specs = (
        P(None, "dp"),
        P("dp", "tensor", None),
        P("dp", "tensor"),
        P("dp", "tensor", None),
        P("dp", "tensor", None),
        P("dp"),
        P("dp", "tensor", None),
    )
    out_specs = (
        P("dp", "tensor", None),
        P("dp", "tensor", None),
        P("dp", "tensor", None),
        P("tensor", "dp"),
        P("dp", "tensor", None),
    )
    return jax.shard_map(body, mesh=mesh, in_specs=in_specs, out_specs=out_specs, check_vma=False)
```

```python
import functools
import math

import jax
import jax.numpy as jnp
from jax import lax
from jax.experimental import pallas as pl
from jax.experimental.pallas import tpu as pltpu
from jax.sharding import PartitionSpec as P

SPAN = 4
Z = 8
YX = 8
F32 = jnp.float32
BF16 = jnp.bfloat16
NT = (((1,), (1,)), ((), ()))
NN = (((1,), (0,)), ((), ()))

Z_GROUPS = [[a * Z + z for z in range(Z)] for a in range(YX)]
YX_GROUPS = [[a * Z + z for a in range(YX)] for z in range(Z)]

tie = lax.optimization_barrier


def shifted(value, steps):
    count = lax.axis_size("dp")
    first, last = (max(0, -steps), min(count, count - steps))
    return lax.ppermute(value, "dp", [(source, source + steps) for source in range(first, last)])


def swap_all(value, groups):
    return lax.all_to_all(value, "dp", 0, 0, tiled=True, axis_index_groups=groups)


def copies(value, count):
    return jnp.broadcast_to(value[None], (count,) + value.shape).reshape(
        (count * value.shape[0],) + value.shape[1:]
    )


def mm(a, b, dims):
    return lax.dot_general(a, b, dims, preferred_element_type=F32)


def fill_window(win, own, h1, h2, h34):
    tok = own.shape[0]
    win[0:tok] = h34[tok:]
    win[tok : 2 * tok] = h34[:tok]
    win[2 * tok : 3 * tok] = h2[...]
    win[3 * tok : 4 * tok] = h1[...]
    win[4 * tok :] = own[...]


def masked_scores(factor, first, win, q_g, start):
    keys = win.shape[0]
    tok = q_g.shape[0]
    key_pos = first - SPAN * tok + lax.broadcasted_iota(jnp.int32, (keys, tok), 0)
    query_pos = first + lax.broadcasted_iota(jnp.int32, (keys, tok), 1)
    allowed = (key_pos >= start) & (key_pos <= query_pos)
    return jnp.where(allowed, mm(win, q_g, NT) * factor, -1e30)


def add_to(acc, part, first):
    if first:
        acc[...] = part
    else:
        acc[...] += part


def store_grads(acc, own, g12, g34):
    tok = own.shape[0]
    own[...] = acc[4 * tok :]
    g12[0:tok] = acc[3 * tok : 4 * tok]
    g12[tok:] = acc[2 * tok : 3 * tok]
    g34[0:tok] = acc[tok : 2 * tok].astype(BF16)
    g34[tok:] = acc[0:tok].astype(BF16)


def probs_kernel(
    factor, base, q, do, k0, k1, k2, k34, start, unused, lse, dv_own, dv12, dv34, kwin, acc
):
    width = k0.shape[1]
    fill_window(kwin, k0, k1, k2, k34)
    for g in range(q.shape[1] // width):
        cols = slice(g * width, (g + 1) * width)
        scores = masked_scores(factor, base[0], kwin[...], q[:, cols], start[...])
        top = jnp.max(scores, axis=0, keepdims=True)
        e = jnp.exp(scores - top)
        total = jnp.sum(e, axis=0, keepdims=True)
        lse[g : g + 1] = top + jnp.log(total)
        p = (e * (1.0 / total)).astype(BF16)
        add_to(acc, mm(p, do[:, cols], NN), g == 0)
    store_grads(acc, dv_own, dv12, dv34)


def attention_kernel(
    factor, base, q, do, k0, k1, k2, k34, v0, v1, v2, v34, start, lse,
    out, dq, dk_own, dk12, dk34, kwin, vwin, acc,
):
    width = k0.shape[1]
    fill_window(kwin, k0, k1, k2, k34)
    fill_window(vwin, v0, v1, v2, v34)
    k_cols = kwin[...].T
    v_cols = vwin[...].T
    for g in range(q.shape[1] // width):
        cols = slice(g * width, (g + 1) * width)
        do_g = do[:, cols]
        scores = masked_scores(factor, base[0], kwin[...], q[:, cols], start[...])
        p = jnp.exp(scores - lse[g : g + 1]).astype(BF16)
        attn = mm(v_cols, p, NN).astype(BF16).astype(F32)
        delta = jnp.sum(do_g.astype(F32).T * attn, axis=0, keepdims=True)
        out[:, cols] = attn.T.astype(BF16)
        dprob = mm(vwin[...], do_g, NT)
        ds = (p.astype(F32) * (dprob - delta) * factor).astype(BF16)
        dq[:, cols] = mm(k_cols, ds, NN).T.astype(BF16)
        add_to(acc, mm(ds, q[:, cols], NN), g == 0)
    store_grads(acc, dk_own, dk12, dk34)


def weight_copies_kernel(exponent, codes, out):
    e = exponent[0, 0]
    scale = jnp.float32(0.0)
    for level, power in zip(range(-2, 2), (0.25, 0.5, 1.0, 2.0)):
        scale = jnp.where(e == level, jnp.float32(power), scale)
    w = (codes[...].astype(F32) * scale).astype(BF16)
    for i in range(out.shape[0]):
        out[i] = w


def total_grad(own, r1, r2):
    return (own[...] + r1[...].astype(F32) + r2[...].astype(F32)).astype(BF16)


def input_grad_kernel(w, own, r1, r2, out):
    out[...] = mm(w[...], total_grad(own, r1, r2), NT).astype(BF16)


def weight_grad_kernel(x, own, r1, r2, out):
    out[...] = mm(x[...], total_grad(own, r1, r2), NN).astype(BF16)


def near_kernel(g12, r34, unused, near1, near2):
    tok = near1.shape[0]
    near1[...] = (g12[0:tok] + r34[0:tok].astype(F32)).astype(BF16)
    near2[...] = (g12[tok:] + r34[tok:].astype(F32)).astype(BF16)


def sum_kernel(parts, unused, out):
    total = parts[0].astype(F32)
    for i in range(1, parts.shape[0]):
        total += parts[i].astype(F32)
    out[...] = total.astype(out.dtype)


def body(x, codes, exponents, queries, keys, doc_start, cotangent):
    feat, tok = x.shape
    width = keys.shape[2]
    group = queries.shape[2] // width
    window = (SPAN + 1) * tok
    heads = lax.axis_size("tensor")
    factor = 1.0 / math.sqrt(width)
    base = (lax.axis_index("dp") * tok).astype(jnp.int32).reshape(1)
    vmem = pl.BlockSpec(memory_space=pltpu.VMEM)
    smem = pl.BlockSpec(memory_space=pltpu.SMEM)
    anywhere = pl.BlockSpec(memory_space=pl.ANY)
    params = pltpu.CompilerParams(vmem_limit_bytes=14 * 1024 * 1024)

    k0 = keys[:, 0, :]
    q = queries[:, 0, :]
    do = cotangent[:, 0, :]
    start = doc_start[None, :]

    w_copies = pl.pallas_call(
        weight_copies_kernel,
        out_shape=jax.ShapeDtypeStruct((Z, feat // (Z * YX), width), BF16),
        in_specs=[smem, vmem],
        out_specs=vmem,
        compiler_params=params,
    )(exponents, codes[:, 0, :])
    w_block = swap_all(w_copies.reshape(feat // YX, width), Z_GROUPS)

    k1 = shifted(k0, 1)
    k2 = shifted(k0, 2)
    w_full = swap_all(copies(w_block, YX), YX_GROUPS)
    k34 = shifted(jnp.concatenate([k1, k2], axis=0), 2)
    v0 = lax.dot_general(
        x, w_full, (((0,), (0,)), ((), ())), preferred_element_type=F32
    ).astype(BF16)
    v1 = shifted(v0, 1)
    v2 = shifted(v0, 2)

    grads_shape = [
        jax.ShapeDtypeStruct((tok, width), F32),
        jax.ShapeDtypeStruct((2 * tok, width), F32),
        jax.ShapeDtypeStruct((2 * tok, width), BF16),
    ]
    lse, dv_own, dv12, dv34 = pl.pallas_call(
        functools.partial(probs_kernel, factor),
        out_shape=[jax.ShapeDtypeStruct((group, tok), F32)] + grads_shape,
        in_specs=[smem] + [vmem] * 7 + [anywhere],
        out_specs=[vmem] * 4,
        scratch_shapes=[pltpu.VMEM((window, width), BF16), pltpu.VMEM((window, width), F32)],
        compiler_params=params,
    )(base, q, do, k0, k1, k2, k34, start, v0)


    def near_sum(g12, r34, unused):
        return pl.pallas_call(
            near_kernel,
            out_shape=[jax.ShapeDtypeStruct((tok, width), BF16)] * 2,
            in_specs=[vmem] * 2 + [anywhere],
            out_specs=[vmem] * 2,
            compiler_params=params,
        )(g12, r34, unused)

    r34 = shifted(dv34, -2)
    near1, near2 = near_sum(dv12, r34, v1)
    r1 = shifted(near1, -1)
    r2 = shifted(near2, -2)
    v34 = shifted(jnp.concatenate([v1, v2], axis=0), 2)

    r1, v34 = tie((r1, v34))

    blocks = heads
    same = pl.BlockSpec((tok, width), lambda i: (0, 0))
    d_part = pl.pallas_call(
        input_grad_kernel,
        grid=(blocks,),
        out_shape=jax.ShapeDtypeStruct((feat, tok), BF16),
        in_specs=[pl.BlockSpec((feat // blocks, width), lambda i: (i, 0)), same, same, same],
        out_specs=pl.BlockSpec((feat // blocks, tok), lambda i: (i, 0)),
        compiler_params=params,
    )(w_full, dv_own, r1, r2)
    d_input = lax.psum_scatter(d_part, "tensor", scatter_dimension=0, tiled=True)
    dw_part = pl.pallas_call(
        weight_grad_kernel,
        grid=(blocks,),
        out_shape=jax.ShapeDtypeStruct((feat, width), BF16),
        in_specs=[pl.BlockSpec((feat // blocks, tok), lambda i: (i, 0)), same, same, same],
        out_specs=pl.BlockSpec((feat // blocks, width), lambda i: (i, 0)),
        compiler_params=params,
    )(x, dv_own, r1, r2)

    dw_block = swap_all(dw_part, YX_GROUPS)
    out, dq, dk_own, dk12, dk34 = pl.pallas_call(
        functools.partial(attention_kernel, factor),
        out_shape=[jax.ShapeDtypeStruct((tok, group * width), BF16)] * 2 + grads_shape,
        in_specs=[smem] + [vmem] * 12,
        out_specs=[vmem] * 5,
        scratch_shapes=[
            pltpu.VMEM((window, width), BF16),
            pltpu.VMEM((window, width), BF16),
            pltpu.VMEM((window, width), F32),
        ],
        compiler_params=params,
    )(base, q, do, k0, k1, k2, k34, v0, v1, v2, v34, start, lse)
    dw_block = pl.pallas_call(
        sum_kernel,
        out_shape=jax.ShapeDtypeStruct((feat // YX, width), BF16),
        in_specs=[vmem, anywhere],
        out_specs=vmem,
        compiler_params=params,
    )(dw_block.reshape(YX, feat // YX, width), dk34)
    dw_own = swap_all(dw_block, Z_GROUPS)
    s1, s2 = near_sum(dk12, shifted(dk34, -2), dw_block)
    projection_gradient = pl.pallas_call(
        sum_kernel,
        out_shape=jax.ShapeDtypeStruct((feat // (YX * Z), width), F32),
        in_specs=[vmem, anywhere],
        out_specs=vmem,
        compiler_params=params,
    )(dw_own.reshape(Z, feat // (YX * Z), width), dk34)
    s1 = shifted(s1, -1)
    s2 = shifted(s2, -2)
    d_keys = (
        dk_own + s1.astype(F32) + s2.astype(F32)
    ).astype(BF16)
    return (
        out[:, None, :],
        dq[:, None, :],
        d_keys[:, None, :],
        d_input,
        projection_gradient[:, None, :],
    )


def solution(mesh):
    in_specs = (
        P(None, "dp"),
        P("dp", "tensor", None),
        P("dp", "tensor"),
        P("dp", "tensor", None),
        P("dp", "tensor", None),
        P("dp"),
        P("dp", "tensor", None),
    )
    out_specs = (
        P("dp", "tensor", None),
        P("dp", "tensor", None),
        P("dp", "tensor", None),
        P("tensor", "dp"),
        P("dp", "tensor", None),
    )
    return jax.shard_map(body, mesh=mesh, in_specs=in_specs, out_specs=out_specs, check_vma=False)
```

```python
import functools
import math

import jax
import jax.numpy as jnp
from jax import lax
from jax.experimental import pallas as pl
from jax.experimental.pallas import tpu as pltpu
from jax.sharding import PartitionSpec as P

SPAN = 4
Z = 8
YX = 8
F32 = jnp.float32
BF16 = jnp.bfloat16
NT = (((1,), (1,)), ((), ()))
NN = (((1,), (0,)), ((), ()))

Z_GROUPS = [[a * Z + z for z in range(Z)] for a in range(YX)]
YX_GROUPS = [[a * Z + z for a in range(YX)] for z in range(Z)]

tie = lax.optimization_barrier


def shifted(value, steps):
    count = lax.axis_size("dp")
    first, last = (max(0, -steps), min(count, count - steps))
    return lax.ppermute(value, "dp", [(source, source + steps) for source in range(first, last)])


def swap_all(value, groups):
    return lax.all_to_all(value, "dp", 0, 0, tiled=True, axis_index_groups=groups)


def copies(value, count):
    return jnp.broadcast_to(value[None], (count,) + value.shape).reshape(
        (count * value.shape[0],) + value.shape[1:]
    )


def mm(a, b, dims):
    return lax.dot_general(a, b, dims, preferred_element_type=F32)


def window_parts(win, own, h1, h2, h34):
    tok = own.shape[0]
    return [
        (own, win.at[4 * tok : 5 * tok]),
        (h1, win.at[3 * tok : 4 * tok]),
        (h2, win.at[2 * tok : 3 * tok]),
        (h34.at[0:tok], win.at[tok : 2 * tok]),
        (h34.at[tok : 2 * tok], win.at[0:tok]),
    ]


def fetch(parts, sems):
    moves = [pltpu.make_async_copy(a, b, sems.at[i]) for i, (a, b) in enumerate(parts)]
    for move in moves:
        move.start()
    for move in moves:
        move.wait()


def masked_scores(factor, first, win, q_g, start):
    keys = win.shape[0]
    tok = q_g.shape[0]
    key_pos = first - SPAN * tok + lax.broadcasted_iota(jnp.int32, (keys, tok), 0)
    query_pos = first + lax.broadcasted_iota(jnp.int32, (keys, tok), 1)
    allowed = (key_pos >= start) & (key_pos <= query_pos)
    return jnp.where(allowed, mm(win, q_g, NT) * factor, -1e30)


def add_to(acc, part, first):
    if first:
        acc[...] = part
    else:
        acc[...] += part


def store_grads(acc, own, g12, g34):
    tok = own.shape[0]
    own[...] = acc[4 * tok :]
    g12[0:tok] = acc[3 * tok : 4 * tok]
    g12[tok:] = acc[2 * tok : 3 * tok]
    g34[0:tok] = acc[tok : 2 * tok].astype(BF16)
    g34[tok:] = acc[0:tok].astype(BF16)


def probs_kernel(
    factor, base, q_in, do_in, k0, k1, k2, k34, start, unused, lse, dv_own, dv12, dv34,
    q, do, kwin, acc, sems,
):
    width = k0.shape[1]
    fetch([(q_in, q), (do_in, do)] + window_parts(kwin, k0, k1, k2, k34), sems)
    for g in range(q.shape[1] // width):
        cols = slice(g * width, (g + 1) * width)
        scores = masked_scores(factor, base[0], kwin[...], q[:, cols], start[...])
        top = jnp.max(scores, axis=0, keepdims=True)
        e = jnp.exp(scores - top)
        total = jnp.sum(e, axis=0, keepdims=True)
        lse[g : g + 1] = top + jnp.log(total)
        p = (e * (1.0 / total)).astype(BF16)
        add_to(acc, mm(p, do[:, cols], NN), g == 0)
    store_grads(acc, dv_own, dv12, dv34)


def attention_kernel(
    factor, base, q_in, do_in, k0, k1, k2, k34, v0, v1, v2, v34, start, lse,
    out, dq, dk_own, dk12, dk34, q, do, kwin, vwin, acc, sems,
):
    width = k0.shape[1]
    fetch(
        [(q_in, q), (do_in, do)]
        + window_parts(kwin, k0, k1, k2, k34)
        + window_parts(vwin, v0, v1, v2, v34),
        sems,
    )
    k_cols = kwin[...].T
    v_cols = vwin[...].T
    for g in range(q.shape[1] // width):
        cols = slice(g * width, (g + 1) * width)
        do_g = do[:, cols]
        scores = masked_scores(factor, base[0], kwin[...], q[:, cols], start[...])
        p = jnp.exp(scores - lse[g : g + 1]).astype(BF16)
        attn = mm(v_cols, p, NN).astype(BF16).astype(F32)
        delta = jnp.sum(do_g.astype(F32).T * attn, axis=0, keepdims=True)
        out[:, cols] = attn.T.astype(BF16)
        dprob = mm(vwin[...], do_g, NT)
        ds = (p.astype(F32) * (dprob - delta) * factor).astype(BF16)
        dq[:, cols] = mm(k_cols, ds, NN).T.astype(BF16)
        add_to(acc, mm(ds, q[:, cols], NN), g == 0)
    store_grads(acc, dk_own, dk12, dk34)


def weight_copies_kernel(exponent, codes, out):
    e = exponent[0, 0]
    scale = jnp.float32(0.0)
    for level, power in zip(range(-2, 2), (0.25, 0.5, 1.0, 2.0)):
        scale = jnp.where(e == level, jnp.float32(power), scale)
    w = (codes[...].astype(F32) * scale).astype(BF16)
    for i in range(out.shape[0]):
        out[i] = w


def value_grad_kernel(x, w, own, r1, r2, d_in, d_w):
    total = (own[...] + r1[...].astype(F32) + r2[...].astype(F32)).astype(BF16)
    d_in[...] = mm(w[...], total, NT).astype(BF16)
    d_w[...] = mm(x[...], total, NN).astype(BF16)


def near_kernel(g12, r34, unused, near1, near2):
    tok = near1.shape[0]
    near1[...] = (g12[0:tok] + r34[0:tok].astype(F32)).astype(BF16)
    near2[...] = (g12[tok:] + r34[tok:].astype(F32)).astype(BF16)


def total_kernel(own, r1, r2, unused, out):
    out[...] = (own[...] + r1[...].astype(F32) + r2[...].astype(F32)).astype(BF16)


def sum_kernel(parts, unused, out):
    total = parts[0].astype(F32)
    for i in range(1, parts.shape[0]):
        total += parts[i].astype(F32)
    out[...] = total.astype(out.dtype)


def body(x, codes, exponents, queries, keys, doc_start, cotangent):
    feat, tok = x.shape
    width = keys.shape[2]
    group = queries.shape[2] // width
    window = (SPAN + 1) * tok
    heads = lax.axis_size("tensor")
    factor = 1.0 / math.sqrt(width)
    base = (lax.axis_index("dp") * tok).astype(jnp.int32).reshape(1)
    vmem = pl.BlockSpec(memory_space=pltpu.VMEM)
    smem = pl.BlockSpec(memory_space=pltpu.SMEM)
    anywhere = pl.BlockSpec(memory_space=pl.ANY)
    hbm = pl.BlockSpec(memory_space=pltpu.HBM)
    params = pltpu.CompilerParams(vmem_limit_bytes=14 * 1024 * 1024)

    k0 = keys[:, 0, :]
    q = queries[:, 0, :]
    do = cotangent[:, 0, :]
    start = doc_start[None, :]

    w_copies = pl.pallas_call(
        weight_copies_kernel,
        out_shape=jax.ShapeDtypeStruct((Z, feat // (Z * YX), width), BF16),
        in_specs=[smem, vmem],
        out_specs=vmem,
        compiler_params=params,
    )(exponents, codes[:, 0, :])
    w_block = swap_all(w_copies.reshape(feat // YX, width), Z_GROUPS)

    k1 = shifted(k0, 1)
    k2 = shifted(k0, 2)
    w_full = swap_all(copies(w_block, YX), YX_GROUPS)
    k34 = shifted(jnp.concatenate([k1, k2], axis=0), 2)
    v0 = lax.dot_general(
        x, w_full, (((0,), (0,)), ((), ())), preferred_element_type=F32
    ).astype(BF16)
    v1 = shifted(v0, 1)
    v2 = shifted(v0, 2)

    grads_shape = [
        jax.ShapeDtypeStruct((tok, width), F32),
        jax.ShapeDtypeStruct((2 * tok, width), F32),
        jax.ShapeDtypeStruct((2 * tok, width), BF16),
    ]
    lse, dv_own, dv12, dv34 = pl.pallas_call(
        functools.partial(probs_kernel, factor),
        out_shape=[jax.ShapeDtypeStruct((group, tok), F32)] + grads_shape,
        in_specs=[smem] + [hbm] * 6 + [vmem, anywhere],
        out_specs=[vmem] * 4,
        scratch_shapes=[
            pltpu.VMEM((tok, group * width), BF16),
            pltpu.VMEM((tok, group * width), BF16),
            pltpu.VMEM((window, width), BF16),
            pltpu.VMEM((window, width), F32),
            pltpu.SemaphoreType.DMA((7,)),
        ],
        compiler_params=params,
    )(base, q, do, k0, k1, k2, k34, start, v0)


    def near_sum(g12, r34, unused):
        return pl.pallas_call(
            near_kernel,
            out_shape=[jax.ShapeDtypeStruct((tok, width), BF16)] * 2,
            in_specs=[vmem] * 2 + [anywhere],
            out_specs=[vmem] * 2,
            compiler_params=params,
        )(g12, r34, unused)

    r34 = shifted(dv34, -2)
    near1, near2 = near_sum(dv12, r34, v1)
    r1 = shifted(near1, -1)
    r2 = shifted(near2, -2)
    v34 = shifted(jnp.concatenate([v1, v2], axis=0), 2)

    r1, v34 = tie((r1, v34))

    blocks = 4
    same = pl.BlockSpec((tok, width), lambda i: (0, 0))
    wide = pl.BlockSpec((feat // blocks, tok), lambda i: (i, 0))
    narrow = pl.BlockSpec((feat // blocks, width), lambda i: (i, 0))
    d_part, dw_part = pl.pallas_call(
        value_grad_kernel,
        grid=(blocks,),
        out_shape=[
            jax.ShapeDtypeStruct((feat, tok), BF16),
            jax.ShapeDtypeStruct((feat, width), BF16),
        ],
        in_specs=[wide, narrow, same, same, same],
        out_specs=[wide, narrow],
        compiler_params=params,
    )(x, w_full, dv_own, r1, r2)
    d_input = lax.psum_scatter(d_part, "tensor", scatter_dimension=0, tiled=True)

    dw_block = swap_all(dw_part, YX_GROUPS)
    out, dq, dk_own, dk12, dk34 = pl.pallas_call(
        functools.partial(attention_kernel, factor),
        out_shape=[jax.ShapeDtypeStruct((tok, group * width), BF16)] * 2 + grads_shape,
        in_specs=[smem] + [hbm] * 6 + [anywhere] * 4 + [vmem] * 2,
        out_specs=[vmem] * 5,
        scratch_shapes=[
            pltpu.VMEM((tok, group * width), BF16),
            pltpu.VMEM((tok, group * width), BF16),
            pltpu.VMEM((window, width), BF16),
            pltpu.VMEM((window, width), BF16),
            pltpu.VMEM((window, width), F32),
            pltpu.SemaphoreType.DMA((12,)),
        ],
        compiler_params=params,
    )(base, q, do, k0, k1, k2, k34, v0, v1, v2, v34, start, lse)
    dw_block = pl.pallas_call(
        sum_kernel,
        out_shape=jax.ShapeDtypeStruct((feat // YX, width), BF16),
        in_specs=[vmem, anywhere],
        out_specs=vmem,
        compiler_params=params,
    )(dw_block.reshape(YX, feat // YX, width), dk34)
    dw_own = swap_all(dw_block, Z_GROUPS)
    s1, s2 = near_sum(dk12, shifted(dk34, -2), dw_block)
    projection_gradient = pl.pallas_call(
        sum_kernel,
        out_shape=jax.ShapeDtypeStruct((feat // (YX * Z), width), F32),
        in_specs=[vmem, anywhere],
        out_specs=vmem,
        compiler_params=params,
        cost_estimate=pl.CostEstimate(
            flops=0, bytes_accessed=64 * 1024 * 1024, transcendentals=0
        ),
    )(dw_own.reshape(Z, feat // (YX * Z), width), dk34)
    s1 = shifted(s1, -1)
    s2 = shifted(s2, -2)
    d_keys = pl.pallas_call(
        total_kernel,
        out_shape=jax.ShapeDtypeStruct((tok, width), BF16),
        in_specs=[vmem] * 3 + [anywhere],
        out_specs=vmem,
        compiler_params=params,
    )(dk_own, s1, s2, projection_gradient)
    return (
        out[:, None, :],
        dq[:, None, :],
        d_keys[:, None, :],
        d_input,
        projection_gradient[:, None, :],
    )


def solution(mesh):
    in_specs = (
        P(None, "dp"),
        P("dp", "tensor", None),
        P("dp", "tensor"),
        P("dp", "tensor", None),
        P("dp", "tensor", None),
        P("dp"),
        P("dp", "tensor", None),
    )
    out_specs = (
        P("dp", "tensor", None),
        P("dp", "tensor", None),
        P("dp", "tensor", None),
        P("tensor", "dp"),
        P("dp", "tensor", None),
    )
    return jax.shard_map(body, mesh=mesh, in_specs=in_specs, out_specs=out_specs, check_vma=False)
```

```python
import functools
import math

import jax
import jax.numpy as jnp
from jax import lax
from jax.experimental import pallas as pl
from jax.experimental.pallas import tpu as pltpu
from jax.sharding import PartitionSpec as P

SPAN = 4
Z = 8
YX = 8
F32 = jnp.float32
BF16 = jnp.bfloat16
NT = (((1,), (1,)), ((), ()))
NN = (((1,), (0,)), ((), ()))

Z_GROUPS = [[a * Z + z for z in range(Z)] for a in range(YX)]
YX_GROUPS = [[a * Z + z for a in range(YX)] for z in range(Z)]

tie = lax.optimization_barrier


def shifted(value, steps):
    count = lax.axis_size("dp")
    first, last = (max(0, -steps), min(count, count - steps))
    return lax.ppermute(value, "dp", [(source, source + steps) for source in range(first, last)])


def swap_all(value, groups):
    return lax.all_to_all(value, "dp", 0, 0, tiled=True, axis_index_groups=groups)


def copies(value, count):
    return jnp.broadcast_to(value[None], (count,) + value.shape).reshape(
        (count * value.shape[0],) + value.shape[1:]
    )


def mm(a, b, dims):
    return lax.dot_general(a, b, dims, preferred_element_type=F32)


def window_parts(win, own, *earlier):
    tok = own.shape[0]
    return [
        (ref, win.at[(SPAN - i) * tok : (SPAN - i + 1) * tok])
        for i, ref in enumerate((own, *earlier))
    ]


def fetch(parts, sems):
    moves = [pltpu.make_async_copy(a, b, sems.at[i]) for i, (a, b) in enumerate(parts)]
    for move in moves:
        move.start()
    for move in moves:
        move.wait()


def masked_scores(factor, first, win, q_g, start):
    keys = win.shape[0]
    tok = q_g.shape[0]
    key_pos = first - SPAN * tok + lax.broadcasted_iota(jnp.int32, (keys, tok), 0)
    query_pos = first + lax.broadcasted_iota(jnp.int32, (keys, tok), 1)
    allowed = (key_pos >= start) & (key_pos <= query_pos)
    return jnp.where(allowed, mm(win, q_g, NT) * factor, -1e30)


def add_to(acc, part, first):
    if first:
        acc[...] = part
    else:
        acc[...] += part


def store_grads(acc, own, g12, g34):
    tok = own.shape[0]
    own[...] = acc[4 * tok :]
    g12[0:tok] = acc[3 * tok : 4 * tok]
    g12[tok:] = acc[2 * tok : 3 * tok]
    g34[0:tok] = acc[tok : 2 * tok].astype(BF16)
    g34[tok:] = acc[0:tok].astype(BF16)


def store_each(acc, own, *earlier):
    tok = own.shape[0]
    own[...] = acc[SPAN * tok :]
    for i, ref in enumerate(earlier):
        ref[...] = acc[(SPAN - 1 - i) * tok : (SPAN - i) * tok].astype(BF16)


def probs_kernel(
    factor, base, q_in, do_in, k0, k1, k2, k3, k4, start, unused, lse, dv_own, dv12, dv34,
    q, do, kwin, acc, sems,
):
    width = k0.shape[1]
    fetch([(q_in, q), (do_in, do)] + window_parts(kwin, k0, k1, k2, k3, k4), sems)
    for g in range(q.shape[1] // width):
        cols = slice(g * width, (g + 1) * width)
        scores = masked_scores(factor, base[0], kwin[...], q[:, cols], start[...])
        top = jnp.max(scores, axis=0, keepdims=True)
        e = jnp.exp(scores - top)
        total = jnp.sum(e, axis=0, keepdims=True)
        lse[g : g + 1] = top + jnp.log(total)
        p = (e * (1.0 / total)).astype(BF16)
        add_to(acc, mm(p, do[:, cols], NN), g == 0)
    store_grads(acc, dv_own, dv12, dv34)


def attention_kernel(
    factor, base, q_in, do_in, k0, k1, k2, k3, k4, v0, v1, v2, v34, start, lse,
    out, dq, dk_own, dk1, dk2, dk3, dk4, q, do, kwin, vwin, acc, sems,
):
    tok, width = k0.shape
    fetch(
        [(q_in, q), (do_in, do)]
        + window_parts(kwin, k0, k1, k2, k3, k4)
        + window_parts(vwin, v0, v1, v2, v34.at[0:tok], v34.at[tok : 2 * tok]),
        sems,
    )
    k_cols = kwin[...].T
    v_cols = vwin[...].T
    for g in range(q.shape[1] // width):
        cols = slice(g * width, (g + 1) * width)
        do_g = do[:, cols]
        scores = masked_scores(factor, base[0], kwin[...], q[:, cols], start[...])
        p = jnp.exp(scores - lse[g : g + 1]).astype(BF16)
        attn = mm(v_cols, p, NN).astype(BF16).astype(F32)
        delta = jnp.sum(do_g.astype(F32).T * attn, axis=0, keepdims=True)
        out[:, cols] = attn.T.astype(BF16)
        dprob = mm(vwin[...], do_g, NT)
        ds = (p.astype(F32) * (dprob - delta) * factor).astype(BF16)
        dq[:, cols] = mm(k_cols, ds, NN).T.astype(BF16)
        add_to(acc, mm(ds, q[:, cols], NN), g == 0)
    store_each(acc, dk_own, dk1, dk2, dk3, dk4)


def weight_copies_kernel(exponent, codes, out):
    e = exponent[0, 0]
    scale = jnp.float32(0.0)
    for level, power in zip(range(-2, 2), (0.25, 0.5, 1.0, 2.0)):
        scale = jnp.where(e == level, jnp.float32(power), scale)
    w = (codes[...].astype(F32) * scale).astype(BF16)
    for i in range(out.shape[0]):
        out[i] = w


def value_grad_kernel(x, w, own, r1, r2, d_in, d_w):
    total = (own[...] + r1[...].astype(F32) + r2[...].astype(F32)).astype(BF16)
    d_in[...] = mm(w[...], total, NT).astype(BF16)
    d_w[...] = mm(x[...], total, NN).astype(BF16)


def near_kernel(g12, r34, unused, near1, near2):
    tok = near1.shape[0]
    near1[...] = (g12[0:tok] + r34[0:tok].astype(F32)).astype(BF16)
    near2[...] = (g12[tok:] + r34[tok:].astype(F32)).astype(BF16)


def total_kernel(own, r1, r2, r3, r4, unused, out):
    total = own[...]
    for ref in (r1, r2, r3, r4):
        total = total + ref[...].astype(F32)
    out[...] = total.astype(BF16)


def sum_kernel(parts, unused, out):
    total = parts[0].astype(F32)
    for i in range(1, parts.shape[0]):
        total += parts[i].astype(F32)
    out[...] = total.astype(out.dtype)


def body(x, codes, exponents, queries, keys, doc_start, cotangent):
    feat, tok = x.shape
    width = keys.shape[2]
    group = queries.shape[2] // width
    window = (SPAN + 1) * tok
    heads = lax.axis_size("tensor")
    factor = 1.0 / math.sqrt(width)
    base = (lax.axis_index("dp") * tok).astype(jnp.int32).reshape(1)
    vmem = pl.BlockSpec(memory_space=pltpu.VMEM)
    smem = pl.BlockSpec(memory_space=pltpu.SMEM)
    anywhere = pl.BlockSpec(memory_space=pl.ANY)
    hbm = pl.BlockSpec(memory_space=pltpu.HBM)
    params = pltpu.CompilerParams(vmem_limit_bytes=14 * 1024 * 1024)

    k0 = keys[:, 0, :]
    q = queries[:, 0, :]
    do = cotangent[:, 0, :]
    start = doc_start[None, :]

    w_copies = pl.pallas_call(
        weight_copies_kernel,
        out_shape=jax.ShapeDtypeStruct((Z, feat // (Z * YX), width), BF16),
        in_specs=[smem, vmem],
        out_specs=vmem,
        compiler_params=params,
    )(exponents, codes[:, 0, :])
    w_block = swap_all(w_copies.reshape(feat // YX, width), Z_GROUPS)

    k1 = shifted(k0, 1)
    k2 = shifted(k0, 2)
    w_full = swap_all(copies(w_block, YX), YX_GROUPS)
    k3 = shifted(k0, 3)
    k4 = shifted(k0, 4)
    v0 = lax.dot_general(
        x, w_full, (((0,), (0,)), ((), ())), preferred_element_type=F32
    ).astype(BF16)
    v1 = shifted(v0, 1)
    v2 = shifted(v0, 2)

    grads_shape = [
        jax.ShapeDtypeStruct((tok, width), F32),
        jax.ShapeDtypeStruct((2 * tok, width), F32),
        jax.ShapeDtypeStruct((2 * tok, width), BF16),
    ]
    lse, dv_own, dv12, dv34 = pl.pallas_call(
        functools.partial(probs_kernel, factor),
        out_shape=[jax.ShapeDtypeStruct((group, tok), F32)] + grads_shape,
        in_specs=[smem] + [hbm] * 7 + [vmem, anywhere],
        out_specs=[vmem] * 4,
        scratch_shapes=[
            pltpu.VMEM((tok, group * width), BF16),
            pltpu.VMEM((tok, group * width), BF16),
            pltpu.VMEM((window, width), BF16),
            pltpu.VMEM((window, width), F32),
            pltpu.SemaphoreType.DMA((7,)),
        ],
        compiler_params=params,
    )(base, q, do, k0, k1, k2, k3, k4, start, v0)


    def near_sum(g12, r34, unused):
        return pl.pallas_call(
            near_kernel,
            out_shape=[jax.ShapeDtypeStruct((tok, width), BF16)] * 2,
            in_specs=[vmem] * 2 + [anywhere],
            out_specs=[vmem] * 2,
            compiler_params=params,
        )(g12, r34, unused)

    r34 = shifted(dv34, -2)
    near1, near2 = near_sum(dv12, r34, v1)
    r1 = shifted(near1, -1)
    r2 = shifted(near2, -2)
    v34 = shifted(jnp.concatenate([v1, v2], axis=0), 2)

    r1, v34 = tie((r1, v34))

    blocks = 4
    same = pl.BlockSpec((tok, width), lambda i: (0, 0))
    wide = pl.BlockSpec((feat // blocks, tok), lambda i: (i, 0))
    narrow = pl.BlockSpec((feat // blocks, width), lambda i: (i, 0))
    d_part, dw_part = pl.pallas_call(
        value_grad_kernel,
        grid=(blocks,),
        out_shape=[
            jax.ShapeDtypeStruct((feat, tok), BF16),
            jax.ShapeDtypeStruct((feat, width), BF16),
        ],
        in_specs=[wide, narrow, same, same, same],
        out_specs=[wide, narrow],
        compiler_params=params,
    )(x, w_full, dv_own, r1, r2)
    d_input = lax.psum_scatter(d_part, "tensor", scatter_dimension=0, tiled=True)

    dw_block = swap_all(dw_part, YX_GROUPS)
    out, dq, dk_own, *dk_earlier = pl.pallas_call(
        functools.partial(attention_kernel, factor),
        out_shape=[jax.ShapeDtypeStruct((tok, group * width), BF16)] * 2
        + [jax.ShapeDtypeStruct((tok, width), F32)]
        + [jax.ShapeDtypeStruct((tok, width), BF16)] * SPAN,
        in_specs=[smem] + [hbm] * 7 + [anywhere] * 4 + [vmem] * 2,
        out_specs=[vmem] * (3 + SPAN),
        scratch_shapes=[
            pltpu.VMEM((tok, group * width), BF16),
            pltpu.VMEM((tok, group * width), BF16),
            pltpu.VMEM((window, width), BF16),
            pltpu.VMEM((window, width), BF16),
            pltpu.VMEM((window, width), F32),
            pltpu.SemaphoreType.DMA((12,)),
        ],
        compiler_params=params,
    )(base, q, do, k0, k1, k2, k3, k4, v0, v1, v2, v34, start, lse)
    dw_block = pl.pallas_call(
        sum_kernel,
        out_shape=jax.ShapeDtypeStruct((feat // YX, width), BF16),
        in_specs=[vmem, anywhere],
        out_specs=vmem,
        compiler_params=params,
    )(dw_block.reshape(YX, feat // YX, width), dk_own)
    dw_own = swap_all(dw_block, Z_GROUPS)
    projection_gradient = pl.pallas_call(
        sum_kernel,
        out_shape=jax.ShapeDtypeStruct((feat // (YX * Z), width), F32),
        in_specs=[vmem, anywhere],
        out_specs=vmem,
        compiler_params=params,
        cost_estimate=pl.CostEstimate(
            flops=0, bytes_accessed=64 * 1024 * 1024, transcendentals=0
        ),
    )(dw_own.reshape(Z, feat // (YX * Z), width), dk_own)
    dk_far = [shifted(grad, -1 - i) for i, grad in enumerate(dk_earlier)]
    d_keys = pl.pallas_call(
        total_kernel,
        out_shape=jax.ShapeDtypeStruct((tok, width), BF16),
        in_specs=[vmem] * (1 + SPAN) + [anywhere],
        out_specs=vmem,
        compiler_params=params,
    )(dk_own, *dk_far, projection_gradient)
    return (
        out[:, None, :],
        dq[:, None, :],
        d_keys[:, None, :],
        d_input,
        projection_gradient[:, None, :],
    )


def solution(mesh):
    in_specs = (
        P(None, "dp"),
        P("dp", "tensor", None),
        P("dp", "tensor"),
        P("dp", "tensor", None),
        P("dp", "tensor", None),
        P("dp"),
        P("dp", "tensor", None),
    )
    out_specs = (
        P("dp", "tensor", None),
        P("dp", "tensor", None),
        P("dp", "tensor", None),
        P("tensor", "dp"),
        P("dp", "tensor", None),
    )
    return jax.shard_map(body, mesh=mesh, in_specs=in_specs, out_specs=out_specs, check_vma=False)
```
